32 devices in a mesh: ia: 4 (over y, x), ja: 2 (over core), ka: 4 (over z).
Axes of the slice: x: 2, y: 2, z: 4, core: 2. Of those that a mesh axis runs over, the one named last changes fastest.
Arguments:
- tensor: bfloat16 [4096, 32, 4096], P('ia', 'ka', 'ja'), may hold values from -64 to 64
- factor_j: bfloat16 [4096, 128], P('ja'), may hold values from -0.0640625 to 0.0640625
- factor_k: bfloat16 [32, 128], P('ka'), may hold values from -0.72478445 to 0.72478445
Outputs:
- core: float32 [128, 32, 4096], P('ia', 'ka', 'ja')
The draws below stay inside these ranges and needn't reach their ends.
All inputs are finite; a program needn't handle non-finite values.
Results may differ from the reference program's by a relative error of at most 0.013.
Values may be sent and summed in bfloat16 or wider, within the bound.
A program may use at most 128 MiB of HBM per device.

```python
import math
import jax
import jax.numpy as jnp
from jax import lax

R = 128
NI = 4096
NJ = 4096
I_DEV = 1024
NK = 32
N_IA = 4


def draw_tensor(key, part):
    keys = jax.random.split(jax.random.fold_in(key, 17), 4)
    base = jnp.clip(jax.random.normal(keys[0], (NI, NK, NJ), jnp.float32), -4.0, 4.0)
    row_scale = jnp.exp(jax.random.uniform(keys[1], (NI, 1, 1), jnp.float32, -1.15, 1.15))
    slice_scale = jnp.exp(jax.random.uniform(keys[2], (1, NK, 1), jnp.float32, -0.6, 0.6))
    col_scale = jnp.exp(jax.random.uniform(keys[3], (1, 1, NJ), jnp.float32, -0.6, 0.6))
    values = base * row_scale * slice_scale * col_scale
    return jnp.clip(values, -64.0, 64.0).astype(jnp.bfloat16)


def factor_values(key, length, width):
    keys = jax.random.split(key, 2)
    own = jnp.clip(jax.random.normal(keys[1], (length, width), jnp.float32), -4.0, 4.0)
    values = own / math.sqrt(length)
    return values


def draw_factor_j(key, part):
    return factor_values(jax.random.fold_in(key, 29), NJ, R).astype(jnp.bfloat16)


def draw_factor_k(key, part):
    return factor_values(jax.random.fold_in(key, 31), NK, R).astype(jnp.bfloat16)


def setup_inputs(seed: int = 0) -> dict:
    splits = jax.random.split(jax.random.key(seed), 4)
    return {
        "tensor": draw_tensor(jax.random.fold_in(splits[3], 71), 0),
        "factor_j": draw_factor_j(jax.random.fold_in(splits[3], 71), 0),
        "factor_k": draw_factor_k(jax.random.fold_in(splits[3], 71), 0),
    }


def reference(tensor, factor_j, factor_k):
    blocks = tensor.reshape(N_IA, I_DEV, NK, NJ)
    weights_k = factor_k.astype(jnp.float32)

    def sketch_block(block):
        mixed = jnp.dot(block.reshape(I_DEV * NK, NJ).astype(jnp.float32), factor_j.astype(jnp.float32), preferred_element_type=jnp.float32)
        return jnp.sum(mixed.reshape(I_DEV, NK, R) * weights_k[None], axis=1)
    sketch = lax.map(sketch_block, blocks).reshape(NI, R)
    basis = sketch
    for sweep in range(2):
        gram = jnp.dot(basis.T.astype(jnp.float32), basis.astype(jnp.float32), precision=lax.Precision.HIGHEST, preferred_element_type=jnp.float32)
        lower = jnp.linalg.cholesky(gram)
        basis = jax.scipy.linalg.solve_triangular(lower, basis.T, lower=True).T
    halves = basis.astype(jnp.bfloat16).reshape(N_IA, I_DEV, R)

    def add_block(total, pair):
        rows_half, block = pair
        term = lax.dot_general(rows_half.astype(jnp.float32), block.reshape(I_DEV, NK * NJ).astype(jnp.float32), (((0,), (0,)), ((), ())), preferred_element_type=jnp.float32)
        term = lax.optimization_barrier(term.astype(jnp.bfloat16)).astype(jnp.float32)
        return (total + term, None)
    core, _ = lax.scan(add_block, jnp.zeros((R, NK * NJ), jnp.float32), (halves, blocks))
    return core.reshape(R, NK, NJ)
```

```python
import functools

import jax
import jax.numpy as jnp
from jax import lax
from jax.experimental import pallas as pl
from jax.experimental.pallas import tpu as pltpu
from jax.sharding import PartitionSpec as P

MESH = pl.DeviceIdType.MESH
F32 = jnp.float32
BF16 = jnp.bfloat16
HIGHEST = lax.Precision.HIGHEST
MIB = 1024 * 1024


def greet(targets):
    barrier = pltpu.get_barrier_semaphore()
    for target in targets:
        pl.semaphore_signal(barrier, inc=1, device_id=target, device_id_type=MESH)
    pl.semaphore_wait(barrier, len(targets))


def sketch_kernel(
    depth, slices, t_ref, fj_ref, fk_ref, out_ref,
    tiles, parts, from_core, from_z, whole,
    load_sems, core_send, core_recv, z_send, z_recv, gz_send, gz_recv, gc_send, gc_recv,
):
    rows = out_ref.shape[0]
    width = out_ref.shape[1]
    share = rows // (2 * depth)
    z, core = lax.axis_index("ka"), lax.axis_index("ja")
    partner = {"ja": 1 - core}
    peers = [lax.rem(z + 1 + s, depth) for s in range(depth - 1)]
    order = [(lax.rem(z + 1 + s, depth), side) for s in range(depth) for side in (1, 0)]

    def offset(owner_z, owner_core):
        return pl.multiple_of((owner_z * 2 + owner_core) * share, share)

    def load(step):
        owner_z, side = order[step]
        owner_core = 1 - core if side else core
        start = pl.multiple_of((owner_z * 2 + owner_core) * share * slices, share * slices)
        return pltpu.make_async_copy(
            t_ref.at[pl.ds(start, share * slices)], tiles.at[step % 3], load_sems.at[step % 3]
        )

    load(0).start()
    load(1).start()
    greet([partner] + [{"ka": peer} for peer in peers])
    weights = fk_ref[...].astype(F32)
    block = min(share, 32)
    core_copies, z_copies = [], []
    for step in range(2 * depth):
        if step + 2 < 2 * depth:
            load(step + 2).start()
        load(step).wait()
        slot = step % 3

        @pl.loop(0, share // block)
        def _(index):
            lines = pl.ds(pl.multiple_of(index * block * slices, block * slices), block * slices)
            mixed = jnp.dot(tiles[slot, lines, :], fj_ref[...], preferred_element_type=F32)
            mixed = mixed.reshape(block, slices, width) * weights[None]
            parts[step, pl.ds(pl.multiple_of(index * block, block), block), :] = jnp.sum(mixed, axis=1)

        hop = step // 2
        if step % 2 == 0:
            copy = pltpu.make_async_remote_copy(
                parts.at[step], from_core.at[hop], core_send.at[hop], core_recv.at[hop],
                device_id=partner, device_id_type=MESH,
            )
            copy.start()
            core_copies.append(copy)
        else:
            core_copies[hop].wait_recv()
            parts[step] = parts[step] + from_core[hop]
            if hop < depth - 1:
                copy = pltpu.make_async_remote_copy(
                    parts.at[step], from_z.at[hop], z_send.at[hop], z_recv.at[hop],
                    device_id={"ka": order[step][0]}, device_id_type=MESH,
                )
                copy.start()
                z_copies.append(copy)

    total = parts[2 * depth - 1]
    for copy, slot in zip(z_copies, range(depth - 1)):
        copy.wait_recv()
        total = total + from_z[slot]
    mine = pl.ds(offset(z, core), share)
    whole[mine, :] = total
    gz = []
    for s, peer in enumerate(peers):
        copy = pltpu.make_async_remote_copy(
            whole.at[mine], whole.at[mine], gz_send.at[s], gz_recv.at[s],
            device_id={"ka": peer}, device_id_type=MESH,
        )
        copy.start()
        gz.append(copy)

    def to_partner(owner, index):
        lines = pl.ds(offset(owner, core), share)
        copy = pltpu.make_async_remote_copy(
            whole.at[lines], whole.at[lines], gc_send.at[index], gc_recv.at[index],
            device_id=partner, device_id_type=MESH,
        )
        copy.start()
        return copy

    gc = [to_partner(z, 0)]
    for s in range(depth - 1):
        gz[s].wait_recv()
        gc.append(to_partner(lax.rem(z + depth - 1 - s, depth), 1 + s))
    for copy in gc:
        copy.wait_recv()
    for copy in core_copies + z_copies + gz + gc:
        copy.wait_send()
    out_ref[...] = whole[...]


def sketch_sum(tensor, factor_j, factor_k, depth):
    rows, slices, columns = tensor.shape
    width = factor_j.shape[1]
    share = rows // (2 * depth)
    dma = lambda n: pltpu.SemaphoreType.DMA((n,))
    return pl.pallas_call(
        functools.partial(sketch_kernel, depth, slices),
        out_shape=jax.ShapeDtypeStruct((rows, width), F32),
        in_specs=[pl.BlockSpec(memory_space=pl.ANY)] + [pl.BlockSpec(memory_space=pltpu.VMEM)] * 2,
        out_specs=pl.BlockSpec(memory_space=pltpu.VMEM),
        scratch_shapes=[
            pltpu.VMEM((3, share * slices, columns), BF16),
            pltpu.VMEM((2 * depth, share, width), F32),
            pltpu.VMEM((depth, share, width), F32),
            pltpu.VMEM((depth, share, width), F32),
            pltpu.VMEM((rows, width), F32),
            dma(3), dma(depth), dma(depth), dma(depth), dma(depth),
            dma(depth), dma(depth), dma(depth), dma(depth),
        ],
        compiler_params=pltpu.CompilerParams(
            collective_id=0, has_side_effects=True, vmem_limit_bytes=40 * MIB
        ),
        cost_estimate=pl.CostEstimate(
            flops=2 * rows * slices * columns * width,
            bytes_accessed=2 * rows * slices * columns, transcendentals=0,
        ),
    )(tensor.reshape(rows * slices, columns), factor_j, factor_k)


def gram_kernel(count, rows_ref, out_ref, grams, send, recv):
    me = lax.axis_index("ia")
    peers = [lax.rem(me + 1 + s, count) for s in range(count - 1)]
    greet([{"ia": peer} for peer in peers])
    value = rows_ref[...]
    grams[me] = lax.dot_general(
        value, value, (((0,), (0,)), ((), ())), precision=HIGHEST, preferred_element_type=F32
    )
    copies = []
    for s, peer in enumerate(peers):
        copy = pltpu.make_async_remote_copy(
            grams.at[me], grams.at[me], send.at[s], recv.at[s],
            device_id={"ia": peer}, device_id_type=MESH,
        )
        copy.start()
        copies.append(copy)
    for copy in copies:
        copy.wait_recv()
    total = grams[0]
    for index in range(1, count):
        total = total + grams[index]
    out_ref[...] = total
    for copy in copies:
        copy.wait_send()


def gram_sum(value, count):
    width = value.shape[1]
    return pl.pallas_call(
        functools.partial(gram_kernel, count),
        out_shape=jax.ShapeDtypeStruct((width, width), F32),
        in_specs=[pl.BlockSpec(memory_space=pltpu.VMEM)],
        out_specs=pl.BlockSpec(memory_space=pltpu.VMEM),
        scratch_shapes=[
            pltpu.VMEM((count, width, width), F32),
            pltpu.SemaphoreType.DMA((count,)),
            pltpu.SemaphoreType.DMA((count,)),
        ],
        compiler_params=pltpu.CompilerParams(collective_id=1, has_side_effects=True),
    )(value)


def inverse_factor(gram, work):
    width = gram.shape[0]
    work[:, :width] = gram
    lines = lax.broadcasted_iota(jnp.int32, (width, width), 0)
    lanes = lax.broadcasted_iota(jnp.int32, (width, width), 1)
    work[:, width:] = jnp.where(lines == lanes, 1.0, 0.0).astype(F32)
    for first in range(0, width, 8):
        panel = work[first:first + 8, :]
        rows = [panel[k:k + 1, :] for k in range(8)]
        cells = {}
        for k in range(8):
            for i in range(k, 8):
                cells[k, i] = jnp.broadcast_to(
                    panel[k:k + 1, first + i:first + i + 1], (1, 2 * width)
                )
        for k in range(8):
            scale = lax.rsqrt(cells[k, k])
            rows[k] = rows[k] * scale
            lower = [None] * 8
            for i in range(k + 1, 8):
                lower[i] = cells[k, i] * scale
            for i in range(k + 1, 8):
                rows[i] = rows[i] - lower[i] * rows[k]
                for m in range(i, 8):
                    cells[i, m] = cells[i, m] - lower[i] * lower[m]
        done = jnp.concatenate(rows, axis=0)
        work[first:first + 8, :] = done
        if first + 8 < width:
            work[first + 8:, :] = work[first + 8:, :] - lax.dot_general(
                done[:, :width], done, (((0,), (0,)), ((), ())),
                precision=HIGHEST, preferred_element_type=F32,
            )[first + 8:, :]


def apply_kernel(gram_ref, rows_ref, out_ref, work):
    width = gram_ref.shape[0]
    inverse_factor(gram_ref[...], work)
    out_ref[...] = lax.dot_general(
        rows_ref[...], work[:, width:], (((1,), (1,)), ((), ())),
        precision=HIGHEST, preferred_element_type=F32,
    ).astype(out_ref.dtype)


def apply_factor(gram, value, dtype):
    width = gram.shape[0]
    return pl.pallas_call(
        apply_kernel,
        out_shape=jax.ShapeDtypeStruct(value.shape, dtype),
        in_specs=[pl.BlockSpec(memory_space=pltpu.VMEM)] * 2,
        out_specs=pl.BlockSpec(memory_space=pltpu.VMEM),
        scratch_shapes=[pltpu.VMEM((width, 2 * width), F32)],
    )(gram, value)


def project_kernel(count, t_ref, half_ref, out_ref, tiles, parts, landed, load_sems, send, recv):
    rows = half_ref.shape[0]
    width = half_ref.shape[1]
    kept = width // count
    chunk = tiles.shape[2]
    steps = t_ref.shape[1] // chunk
    me = lax.axis_index("ia")
    peers = [lax.rem(me + 1 + s, count) for s in range(count - 1)]
    strip = 512

    def load(step):
        return pltpu.make_async_copy(
            t_ref.at[:, pl.ds(step * chunk, chunk)], tiles.at[step % 2], load_sems.at[step % 2]
        )

    load(0).start()
    greet([{"ia": peer} for peer in peers])
    copies = []
    for step in range(steps):
        if step + 1 < steps:
            load(step + 1).start()
        load(step).wait()

        @pl.loop(0, chunk // strip)
        def _(index):
            cols = pl.ds(pl.multiple_of(index * strip, strip), strip)
            value = lax.dot_general(
                half_ref[...], tiles[step % 2, :, cols], (((0,), (0,)), ((), ())),
                preferred_element_type=F32,
            ).astype(BF16)
            parts[step, :, :, cols] = value.reshape(count, kept, strip)

        for s, peer in enumerate(peers):
            copy = pltpu.make_async_remote_copy(
                parts.at[step, peer], landed.at[step, s], send.at[step, s], recv.at[step, s],
                device_id={"ia": peer}, device_id_type=MESH,
            )
            copy.start()
            copies.append(copy)
    for step in range(steps):
        for s in range(count - 1):
            copies[step * (count - 1) + s].wait_recv()
        total = parts[step, me].astype(F32)
        for s in range(count - 1):
            total = total + landed[step, s].astype(F32)
        out_ref[:, pl.ds(step * chunk, chunk)] = total
    for copy in copies:
        copy.wait_send()


def project(flat, half, count):
    rows, columns = flat.shape
    width = half.shape[1]
    kept = width // count
    chunk = 2048
    steps = columns // chunk
    return pl.pallas_call(
        functools.partial(project_kernel, count),
        out_shape=jax.ShapeDtypeStruct((kept, columns), F32),
        in_specs=[pl.BlockSpec(memory_space=pl.ANY), pl.BlockSpec(memory_space=pltpu.VMEM)],
        out_specs=pl.BlockSpec(memory_space=pltpu.VMEM),
        scratch_shapes=[
            pltpu.VMEM((2, rows, chunk), BF16),
            pltpu.VMEM((steps, count, kept, chunk), BF16),
            pltpu.VMEM((steps, count, kept, chunk), BF16),
            pltpu.SemaphoreType.DMA((2,)),
            pltpu.SemaphoreType.DMA((steps, count)),
            pltpu.SemaphoreType.DMA((steps, count)),
        ],
        compiler_params=pltpu.CompilerParams(
            collective_id=2, has_side_effects=True, vmem_limit_bytes=48 * MIB
        ),
        cost_estimate=pl.CostEstimate(
            flops=2 * rows * columns * width, bytes_accessed=2 * rows * columns, transcendentals=0,
        ),
    )(flat, half)


def shards(tensor, factor_j, factor_k):
    rows, slices, columns = tensor.shape
    count, depth = lax.axis_size("ia"), lax.axis_size("ka")
    sketch = sketch_sum(tensor, factor_j, factor_k, depth)
    basis = apply_factor(gram_sum(sketch, count), sketch, F32)
    half = apply_factor(gram_sum(basis, count), basis, BF16)
    core = project(tensor.reshape(rows, slices * columns), half, count)
    return core.reshape(core.shape[0], slices, columns)


def solution(mesh):
    return jax.shard_map(
        shards,
        mesh=mesh,
        in_specs=(P("ia", "ka", "ja"), P("ja", None), P("ka", None)),
        out_specs=P("ia", "ka", "ja"),
        check_vma=False,
    )
```

```python
import functools

import jax
import jax.numpy as jnp
from jax import lax
from jax.experimental import pallas as pl
from jax.experimental.pallas import tpu as pltpu
from jax.sharding import PartitionSpec as P

MESH = pl.DeviceIdType.MESH
F32 = jnp.float32
BF16 = jnp.bfloat16
HIGHEST = lax.Precision.HIGHEST
MIB = 1024 * 1024


def greet(targets):
    barrier = pltpu.get_barrier_semaphore()
    for target in targets:
        pl.semaphore_signal(barrier, inc=1, device_id=target, device_id_type=MESH)
    pl.semaphore_wait(barrier, len(targets))


def sketch_kernel(
    depth, slices, t_ref, fj_ref, fk_ref, out_ref,
    tiles, parts, from_core, from_z, whole,
    load_sems, core_send, core_recv, z_send, z_recv, gz_send, gz_recv, gc_send, gc_recv,
):
    rows = out_ref.shape[0]
    width = out_ref.shape[1]
    share = rows // (2 * depth)
    z, core = lax.axis_index("ka"), lax.axis_index("ja")
    partner = {"ja": 1 - core}
    peers = [lax.rem(z + 1 + s, depth) for s in range(depth - 1)]
    order = [(lax.rem(z + 1 + s, depth), side) for s in range(depth) for side in (1, 0)]

    def offset(owner_z, owner_core):
        return pl.multiple_of((owner_z * 2 + owner_core) * share, share)

    def load(step):
        owner_z, side = order[step]
        owner_core = 1 - core if side else core
        start = pl.multiple_of((owner_z * 2 + owner_core) * share * slices, share * slices)
        return pltpu.make_async_copy(
            t_ref.at[pl.ds(start, share * slices)], tiles.at[step % 3], load_sems.at[step % 3]
        )

    load(0).start()
    load(1).start()
    greet([partner] + [{"ka": peer} for peer in peers])
    weights = fk_ref[...].astype(F32)
    block = min(share, 32)
    core_copies, z_copies = [], []
    for step in range(2 * depth):
        if step + 2 < 2 * depth:
            load(step + 2).start()
        load(step).wait()
        slot = step % 3

        @pl.loop(0, share // block)
        def _(index):
            lines = pl.ds(pl.multiple_of(index * block * slices, block * slices), block * slices)
            mixed = jnp.dot(tiles[slot, lines, :], fj_ref[...], preferred_element_type=F32)
            mixed = mixed.reshape(block, slices, width) * weights[None]
            parts[step, pl.ds(pl.multiple_of(index * block, block), block), :] = jnp.sum(mixed, axis=1)

        hop = step // 2
        if step % 2 == 0:
            copy = pltpu.make_async_remote_copy(
                parts.at[step], from_core.at[hop], core_send.at[hop], core_recv.at[hop],
                device_id=partner, device_id_type=MESH,
            )
            copy.start()
            core_copies.append(copy)
        else:
            core_copies[hop].wait_recv()
            parts[step] = parts[step] + from_core[hop]
            if hop < depth - 1:
                copy = pltpu.make_async_remote_copy(
                    parts.at[step], from_z.at[hop], z_send.at[hop], z_recv.at[hop],
                    device_id={"ka": order[step][0]}, device_id_type=MESH,
                )
                copy.start()
                z_copies.append(copy)

    total = parts[2 * depth - 1]
    for copy, slot in zip(z_copies, range(depth - 1)):
        copy.wait_recv()
        total = total + from_z[slot]
    mine = pl.ds(offset(z, core), share)
    whole[mine, :] = total
    gz = []
    for s, peer in enumerate(peers):
        copy = pltpu.make_async_remote_copy(
            whole.at[mine], whole.at[mine], gz_send.at[s], gz_recv.at[s],
            device_id={"ka": peer}, device_id_type=MESH,
        )
        copy.start()
        gz.append(copy)

    def to_partner(owner, index):
        lines = pl.ds(offset(owner, core), share)
        copy = pltpu.make_async_remote_copy(
            whole.at[lines], whole.at[lines], gc_send.at[index], gc_recv.at[index],
            device_id=partner, device_id_type=MESH,
        )
        copy.start()
        return copy

    gc = [to_partner(z, 0)]
    for s in range(depth - 1):
        gz[s].wait_recv()
        gc.append(to_partner(lax.rem(z + depth - 1 - s, depth), 1 + s))
    for copy in gc:
        copy.wait_recv()
    for copy in core_copies + z_copies + gz + gc:
        copy.wait_send()
    out_ref[...] = whole[...]


def sketch_sum(tensor, factor_j, factor_k, depth):
    rows, slices, columns = tensor.shape
    width = factor_j.shape[1]
    share = rows // (2 * depth)
    dma = lambda n: pltpu.SemaphoreType.DMA((n,))
    return pl.pallas_call(
        functools.partial(sketch_kernel, depth, slices),
        out_shape=jax.ShapeDtypeStruct((rows, width), F32),
        in_specs=[pl.BlockSpec(memory_space=pl.ANY)] + [pl.BlockSpec(memory_space=pltpu.VMEM)] * 2,
        out_specs=pl.BlockSpec(memory_space=pltpu.VMEM),
        scratch_shapes=[
            pltpu.VMEM((3, share * slices, columns), BF16),
            pltpu.VMEM((2 * depth, share, width), F32),
            pltpu.VMEM((depth, share, width), F32),
            pltpu.VMEM((depth, share, width), F32),
            pltpu.VMEM((rows, width), F32),
            dma(3), dma(depth), dma(depth), dma(depth), dma(depth),
            dma(depth), dma(depth), dma(depth), dma(depth),
        ],
        compiler_params=pltpu.CompilerParams(
            collective_id=0, has_side_effects=True, vmem_limit_bytes=40 * MIB
        ),
        cost_estimate=pl.CostEstimate(
            flops=2 * rows * slices * columns * width,
            bytes_accessed=2 * rows * slices * columns, transcendentals=0,
        ),
    )(tensor.reshape(rows * slices, columns), factor_j, factor_k)


def gram_kernel(count, rows_ref, out_ref, grams, send, recv):
    me = lax.axis_index("ia")
    peers = [lax.rem(me + 1 + s, count) for s in range(count - 1)]
    greet([{"ia": peer} for peer in peers])
    value = rows_ref[...]
    grams[me] = lax.dot_general(
        value, value, (((0,), (0,)), ((), ())), precision=HIGHEST, preferred_element_type=F32
    )
    copies = []
    for s, peer in enumerate(peers):
        copy = pltpu.make_async_remote_copy(
            grams.at[me], grams.at[me], send.at[s], recv.at[s],
            device_id={"ia": peer}, device_id_type=MESH,
        )
        copy.start()
        copies.append(copy)
    for copy in copies:
        copy.wait_recv()
    total = grams[0]
    for index in range(1, count):
        total = total + grams[index]
    out_ref[...] = total
    for copy in copies:
        copy.wait_send()


def gram_sum(value, count):
    width = value.shape[1]
    return pl.pallas_call(
        functools.partial(gram_kernel, count),
        out_shape=jax.ShapeDtypeStruct((width, width), F32),
        in_specs=[pl.BlockSpec(memory_space=pltpu.VMEM)],
        out_specs=pl.BlockSpec(memory_space=pltpu.VMEM),
        scratch_shapes=[
            pltpu.VMEM((count, width, width), F32),
            pltpu.SemaphoreType.DMA((count,)),
            pltpu.SemaphoreType.DMA((count,)),
        ],
        compiler_params=pltpu.CompilerParams(collective_id=1, has_side_effects=True),
    )(value)


def inverse_factor(gram, work):
    width = gram.shape[0]
    work[:, :width] = gram
    lines = lax.broadcasted_iota(jnp.int32, (width, width), 0)
    lanes = lax.broadcasted_iota(jnp.int32, (width, width), 1)
    work[:, width:] = jnp.where(lines == lanes, 1.0, 0.0).astype(F32)
    for first in range(0, width, 8):
        panel = work[first:first + 8, :]
        rows = [panel[k:k + 1, :] for k in range(8)]
        cells = {}
        for k in range(8):
            for i in range(k, 8):
                cells[k, i] = jnp.broadcast_to(
                    panel[k:k + 1, first + i:first + i + 1], (1, 2 * width)
                )
        for k in range(8):
            scale = lax.rsqrt(cells[k, k])
            rows[k] = rows[k] * scale
            lower = [None] * 8
            for i in range(k + 1, 8):
                lower[i] = cells[k, i] * scale
            for i in range(k + 1, 8):
                rows[i] = rows[i] - lower[i] * rows[k]
                for m in range(i, 8):
                    cells[i, m] = cells[i, m] - lower[i] * lower[m]
        done = jnp.concatenate(rows, axis=0)
        work[first:first + 8, :] = done
        if first + 8 < width:
            work[first + 8:, :] = work[first + 8:, :] - lax.dot_general(
                done[:, :width], done, (((0,), (0,)), ((), ())),
                precision=HIGHEST, preferred_element_type=F32,
            )[first + 8:, :]


def apply_kernel(flip, gram_ref, rows_ref, out_ref, work):
    width = gram_ref.shape[0]
    inverse_factor(gram_ref[...], work)
    left, right = rows_ref[...], work[:, width:]
    if flip:
        left, right = right, left
    out_ref[...] = lax.dot_general(
        left, right, (((1,), (1,)), ((), ())), precision=HIGHEST, preferred_element_type=F32
    ).astype(out_ref.dtype)


def apply_factor(gram, value, flip, dtype):
    width = gram.shape[0]
    return pl.pallas_call(
        functools.partial(apply_kernel, flip),
        out_shape=jax.ShapeDtypeStruct(value.shape[::-1] if flip else value.shape, dtype),
        in_specs=[pl.BlockSpec(memory_space=pltpu.VMEM)] * 2,
        out_specs=pl.BlockSpec(memory_space=pltpu.VMEM),
        scratch_shapes=[pltpu.VMEM((width, 2 * width), F32)],
    )(gram, value)


def project_kernel(
    count, t_ref, half_ref, out_ref, tiles, perm, turned, parts, landed, load_sems, send, recv
):
    rows = half_ref.shape[1]
    kept, slices, columns = out_ref.shape
    strip = tiles.shape[2]
    steps = columns // strip
    group = perm.shape[0] // slices
    me = lax.axis_index("ia")
    if count == 4:
        x, y = lax.rem(me, 2), me // 2
        x_near, y_near, far = me + 1 - 2 * x, me + 2 - 4 * y, 3 - me
        peers = [x_near, y_near]
    else:
        peers = [lax.rem(me + 1 + s, count) for s in range(count - 1)]

    def load(step):
        return pltpu.make_async_copy(
            t_ref.at[:, pl.ds(step * strip, strip)], tiles.at[step % 2], load_sems.at[step % 2]
        )

    def push(source, step, slot, target):
        copy = pltpu.make_async_remote_copy(
            parts.at[step, source], landed.at[step, slot], send.at[step, slot], recv.at[step, slot],
            device_id={"ia": target}, device_id_type=MESH,
        )
        copy.start()
        return copy

    load(0).start()
    line = lax.broadcasted_iota(jnp.int32, perm.shape, 0)
    lane = lax.broadcasted_iota(jnp.int32, perm.shape, 1)
    perm[...] = jnp.where(
        lane == lax.rem(line, group) * slices + lax.div(line, group), 1.0, 0.0
    ).astype(BF16)
    greet([{"ia": peer} for peer in peers])
    copies = {}

    def near(step):
        return (x_near, y_near) if step % 2 == 0 else (y_near, x_near)

    def relay(step):
        second = near(step)[1]
        copies[step, 1].wait_recv()
        added = parts[step, second].astype(F32) + landed[step, 1].astype(F32)
        parts[step, second] = added.astype(BF16)
        copies[step, 2] = push(second, step, 2, second)

    def finish(step):
        slots = (0, 2) if count == 4 else range(count - 1)
        total = parts[step, me].astype(F32)
        for slot in slots:
            copies[step, slot].wait_recv()
            total = total + landed[step, slot].astype(F32)
        for k in range(slices):
            out_ref[:, k, pl.ds(step * strip, strip)] = total[:, k * strip:(k + 1) * strip]

    for step in range(steps):
        if step + 1 < steps:
            load(step + 1).start()
        load(step).wait()

        @pl.loop(0, rows // group, unroll=4)
        def _(index):
            span = group * slices
            lines = pl.ds(pl.multiple_of(index * span, span), span)
            value = jnp.dot(perm[...], tiles[step % 2, lines, :], preferred_element_type=F32)
            value = value.astype(BF16)
            for k in range(slices):
                place = pl.ds(pl.multiple_of(index * group, group), group)
                turned[k, place, :] = value[k * group:(k + 1) * group]

        @pl.loop(0, slices, unroll=2)
        def _(k):
            value = jnp.dot(half_ref[...], turned[k], preferred_element_type=F32).astype(BF16)
            cols = pl.ds(pl.multiple_of(k * strip, strip), strip)
            parts[step, :, :, cols] = value.reshape(count, kept, strip)

        if count == 4:
            first = near(step)[0]
            copies[step, 1] = push(far, step, 1, first)
            copies[step, 0] = push(first, step, 0, first)
            if step >= 1:
                relay(step - 1)
        else:
            for s, peer in enumerate(peers):
                copies[step, s] = push(peer, step, s, peer)
        if step >= 4:
            finish(step - 4)
    if count == 4:
        relay(steps - 1)
    for step in range(max(steps - 4, 0), steps):
        finish(step)
    for copy in copies.values():
        copy.wait_send()


def project(tensor, half, count):
    rows, slices, columns = tensor.shape
    width = half.shape[0]
    kept = width // count
    strip = 256
    steps = columns // strip
    group = max(256 // slices, 16)
    return pl.pallas_call(
        functools.partial(project_kernel, count),
        out_shape=jax.ShapeDtypeStruct((kept, slices, columns), F32),
        in_specs=[pl.BlockSpec(memory_space=pl.ANY), pl.BlockSpec(memory_space=pltpu.VMEM)],
        out_specs=pl.BlockSpec(memory_space=pltpu.VMEM),
        scratch_shapes=[
            pltpu.VMEM((2, rows * slices, strip), BF16),
            pltpu.VMEM((group * slices, group * slices), BF16),
            pltpu.VMEM((slices, rows, strip), BF16),
            pltpu.VMEM((steps, count, kept, slices * strip), BF16),
            pltpu.VMEM((steps, count, kept, slices * strip), BF16),
            pltpu.SemaphoreType.DMA((2,)),
            pltpu.SemaphoreType.DMA((steps, count)),
            pltpu.SemaphoreType.DMA((steps, count)),
        ],
        compiler_params=pltpu.CompilerParams(
            collective_id=2, has_side_effects=True, vmem_limit_bytes=48 * MIB
        ),
        cost_estimate=pl.CostEstimate(
            flops=2 * rows * slices * columns * width,
            bytes_accessed=2 * rows * slices * columns, transcendentals=0,
        ),
    )(tensor.reshape(rows * slices, columns), half)


def shards(tensor, factor_j, factor_k):
    count, depth = lax.axis_size("ia"), lax.axis_size("ka")
    sketch = sketch_sum(tensor, factor_j, factor_k, depth)
    basis = apply_factor(gram_sum(sketch, count), sketch, False, F32)
    half = apply_factor(gram_sum(basis, count), basis, True, BF16)
    return project(tensor, half, count)


def solution(mesh):
    return jax.shard_map(
        shards,
        mesh=mesh,
        in_specs=(P("ia", "ka", "ja"), P("ja", None), P("ka", None)),
        out_specs=P("ia", "ka", "ja"),
        check_vma=False,
    )
```

```python
import functools

import jax
import jax.numpy as jnp
from jax import lax
from jax.experimental import pallas as pl
from jax.experimental.pallas import tpu as pltpu
from jax.sharding import PartitionSpec as P

MESH = pl.DeviceIdType.MESH
F32 = jnp.float32
BF16 = jnp.bfloat16
HIGHEST = lax.Precision.HIGHEST
MIB = 1024 * 1024


def greet(targets):
    barrier = pltpu.get_barrier_semaphore()
    for target in targets:
        pl.semaphore_signal(barrier, inc=1, device_id=target, device_id_type=MESH)
    pl.semaphore_wait(barrier, len(targets))


def sketch_kernel(
    count, depth, slices, t_ref, fj_hbm, fk_hbm, out_ref, gram_ref,
    tiles, fj_ref, fk_ref, parts, from_core, from_z, whole, grams,
    load_sems, core_send, core_recv, z_send, z_recv, gz_send, gz_recv, gc_send, gc_recv,
    gram_send, gram_recv, factor_sems,
):
    rows = out_ref.shape[0]
    width = out_ref.shape[1]
    share = rows // (2 * depth)
    z, core = lax.axis_index("ka"), lax.axis_index("ja")
    partner = {"ja": 1 - core}
    peers = [lax.rem(z + 1 + s, depth) for s in range(depth - 1)]
    order = [(lax.rem(z + 1 + s, depth), side) for s in range(depth) for side in (1, 0)]

    def offset(owner_z, owner_core):
        return pl.multiple_of((owner_z * 2 + owner_core) * share, share)

    def load(step):
        owner_z, side = order[step]
        owner_core = 1 - core if side else core
        start = pl.multiple_of((owner_z * 2 + owner_core) * share * slices, share * slices)
        return pltpu.make_async_copy(
            t_ref.at[pl.ds(start, share * slices)], tiles.at[step % 3], load_sems.at[step % 3]
        )

    factors = [
        pltpu.make_async_copy(fj_hbm, fj_ref, factor_sems.at[0]),
        pltpu.make_async_copy(fk_hbm, fk_ref, factor_sems.at[1]),
    ]
    for copy in factors:
        copy.start()
    load(0).start()
    load(1).start()
    greet([partner] + [{"ka": peer} for peer in peers] + other_rows(count))
    for copy in factors:
        copy.wait()
    weights = fk_ref[...].astype(F32)
    block = min(share, 32)
    core_copies, z_copies = [], []
    for step in range(2 * depth):
        if step + 2 < 2 * depth:
            load(step + 2).start()
        load(step).wait()
        slot = step % 3

        @pl.loop(0, share // block, unroll=min(share // block, 4))
        def _(index):
            lines = pl.ds(pl.multiple_of(index * block * slices, block * slices), block * slices)
            mixed = jnp.dot(tiles[slot, lines, :], fj_ref[...], preferred_element_type=F32)
            mixed = mixed.reshape(block, slices, width) * weights[None]
            parts[step, pl.ds(pl.multiple_of(index * block, block), block), :] = jnp.sum(mixed, axis=1)

        hop = step // 2
        if step % 2 == 0:
            copy = pltpu.make_async_remote_copy(
                parts.at[step], from_core.at[hop], core_send.at[hop], core_recv.at[hop],
                device_id=partner, device_id_type=MESH,
            )
            copy.start()
            core_copies.append(copy)
        else:
            core_copies[hop].wait_recv()
            parts[step] = parts[step] + from_core[hop]
            if hop < depth - 1:
                copy = pltpu.make_async_remote_copy(
                    parts.at[step], from_z.at[hop], z_send.at[hop], z_recv.at[hop],
                    device_id={"ka": order[step][0]}, device_id_type=MESH,
                )
                copy.start()
                z_copies.append(copy)

    total = parts[2 * depth - 1]
    for copy, slot in zip(z_copies, range(depth - 1)):
        copy.wait_recv()
        total = total + from_z[slot]
    mine = pl.ds(offset(z, core), share)
    whole[mine, :] = total
    gz = []
    for s, peer in enumerate(peers):
        copy = pltpu.make_async_remote_copy(
            whole.at[mine], whole.at[mine], gz_send.at[s], gz_recv.at[s],
            device_id={"ka": peer}, device_id_type=MESH,
        )
        copy.start()
        gz.append(copy)

    def to_partner(owner, index):
        lines = pl.ds(offset(owner, core), share)
        copy = pltpu.make_async_remote_copy(
            whole.at[lines], whole.at[lines], gc_send.at[index], gc_recv.at[index],
            device_id=partner, device_id_type=MESH,
        )
        copy.start()
        return copy

    gc = [to_partner(z, 0)]
    for s in range(depth - 1):
        gz[s].wait_recv()
        gc.append(to_partner(lax.rem(z + depth - 1 - s, depth), 1 + s))
    for copy in gc:
        copy.wait_recv()
    out_ref[...] = whole[...]
    gram_ref[...] = exchange(whole[...], count, grams, gram_send, gram_recv)
    for copy in core_copies + z_copies + gz + gc:
        copy.wait_send()


def sketch_sum(tensor, factor_j, factor_k, count, depth):
    rows, slices, columns = tensor.shape
    width = factor_j.shape[1]
    share = rows // (2 * depth)
    dma = lambda n: pltpu.SemaphoreType.DMA((n,))
    return pl.pallas_call(
        functools.partial(sketch_kernel, count, depth, slices),
        out_shape=[
            jax.ShapeDtypeStruct((rows, width), F32), jax.ShapeDtypeStruct((width, width), F32)
        ],
        in_specs=[pl.BlockSpec(memory_space=pl.ANY)] * 3,
        out_specs=[pl.BlockSpec(memory_space=pltpu.VMEM)] * 2,
        scratch_shapes=[
            pltpu.VMEM((3, share * slices, columns), BF16),
            pltpu.VMEM(factor_j.shape, BF16),
            pltpu.VMEM(factor_k.shape, BF16),
            pltpu.VMEM((2 * depth, share, width), F32),
            pltpu.VMEM((depth, share, width), F32),
            pltpu.VMEM((depth, share, width), F32),
            pltpu.VMEM((rows, width), F32),
            pltpu.VMEM((count, width, width), F32),
            dma(3), dma(depth), dma(depth), dma(depth), dma(depth),
            dma(depth), dma(depth), dma(depth), dma(depth),
            dma(count), dma(count), dma(2),
        ],
        compiler_params=pltpu.CompilerParams(
            collective_id=0, has_side_effects=True, vmem_limit_bytes=40 * MIB
        ),
        cost_estimate=pl.CostEstimate(
            flops=2 * rows * slices * columns * width,
            bytes_accessed=2 * rows * slices * columns, transcendentals=0,
        ),
    )(tensor.reshape(rows * slices, columns), factor_j, factor_k)


def exchange(value, count, grams, send, recv):
    me = lax.axis_index("ia")
    grams[me] = lax.dot_general(
        value, value, (((0,), (0,)), ((), ())), precision=HIGHEST, preferred_element_type=F32
    )
    copies = []
    for s in range(count - 1):
        copy = pltpu.make_async_remote_copy(
            grams.at[me], grams.at[me], send.at[s], recv.at[s],
            device_id={"ia": lax.rem(me + 1 + s, count)}, device_id_type=MESH,
        )
        copy.start()
        copies.append(copy)
    for copy in copies:
        copy.wait_recv()
    total = grams[0]
    for index in range(1, count):
        total = total + grams[index]
    for copy in copies:
        copy.wait_send()
    return total


def other_rows(count):
    me = lax.axis_index("ia")
    return [{"ia": lax.rem(me + 1 + s, count)} for s in range(count - 1)]


def gram_kernel(count, rows_ref, out_ref, grams, send, recv):
    greet(other_rows(count))
    out_ref[...] = exchange(rows_ref[...], count, grams, send, recv)


def gram_sum(value, count):
    width = value.shape[1]
    return pl.pallas_call(
        functools.partial(gram_kernel, count),
        out_shape=jax.ShapeDtypeStruct((width, width), F32),
        in_specs=[pl.BlockSpec(memory_space=pltpu.VMEM)],
        out_specs=pl.BlockSpec(memory_space=pltpu.VMEM),
        scratch_shapes=[
            pltpu.VMEM((count, width, width), F32),
            pltpu.SemaphoreType.DMA((count,)),
            pltpu.SemaphoreType.DMA((count,)),
        ],
        compiler_params=pltpu.CompilerParams(collective_id=1, has_side_effects=True),
    )(value)


def inverse_factor(gram, work):
    width = gram.shape[0]
    work[:, :width] = gram
    lines = lax.broadcasted_iota(jnp.int32, (width, width), 0)
    lanes = lax.broadcasted_iota(jnp.int32, (width, width), 1)
    work[:, width:] = jnp.where(lines == lanes, 1.0, 0.0).astype(F32)

    def cell(row, lane):
        return jnp.broadcast_to(row[:, lane:lane + 1], (1, width))

    def read(first):
        panel = work[first:first + 8, :]
        return [[panel[k:k + 1, :width], panel[k:k + 1, width:]] for k in range(8)]

    rows = read(0)
    for first in range(0, width, 8):
        cells = {(k, i): cell(rows[k][0], first + i) for k in range(8) for i in range(k, 8)}
        for k in range(8):
            scale = lax.rsqrt(cells[k, k])
            rows[k] = [half * scale for half in rows[k]]
            lower = {i: cells[k, i] * scale for i in range(k + 1, 8)}
            for i in range(k + 1, 8):
                rows[i] = [mine - lower[i] * pivot for mine, pivot in zip(rows[i], rows[k])]
                for m in range(i, 8):
                    cells[i, m] = cells[i, m] - lower[i] * lower[m]
        left = jnp.concatenate([row[0] for row in rows], axis=0)
        right = jnp.concatenate([row[1] for row in rows], axis=0)
        work[first:first + 8, :width] = left
        work[first:first + 8, width:] = right
        if first + 8 < width:
            following = read(first + 8)
            for i in range(8):
                for k in range(8):
                    factor = cell(rows[k][0], first + 8 + i)
                    following[i] = [
                        mine - factor * pivot for mine, pivot in zip(following[i], rows[k])
                    ]
            if first + 16 < width:
                done = jnp.concatenate([left, right], axis=1)
                work[first + 16:, :] = work[first + 16:, :] - lax.dot_general(
                    left, done, (((0,), (0,)), ((), ())),
                    precision=HIGHEST, preferred_element_type=F32,
                )[first + 16:, :]
            rows = following


def apply_kernel(flip, gram_ref, rows_ref, out_ref, work):
    width = gram_ref.shape[0]
    inverse_factor(gram_ref[...], work)
    left, right = rows_ref[...], work[:, width:]
    if flip:
        left, right = right, left
    out_ref[...] = lax.dot_general(
        left, right, (((1,), (1,)), ((), ())), precision=HIGHEST, preferred_element_type=F32
    ).astype(out_ref.dtype)


def apply_factor(gram, value, flip, dtype):
    width = gram.shape[0]
    return pl.pallas_call(
        functools.partial(apply_kernel, flip),
        out_shape=jax.ShapeDtypeStruct(value.shape[::-1] if flip else value.shape, dtype),
        in_specs=[pl.BlockSpec(memory_space=pltpu.VMEM)] * 2,
        out_specs=pl.BlockSpec(memory_space=pltpu.VMEM),
        scratch_shapes=[pltpu.VMEM((width, 2 * width), F32)],
    )(gram, value)


def project_kernel(
    count, t_ref, half_ref, out_ref, tiles, perm, turned, parts, landed, load_sems, send, recv
):
    rows = half_ref.shape[1]
    kept, slices, columns = out_ref.shape
    strip = tiles.shape[2]
    steps = columns // strip
    group = perm.shape[0] // slices
    me = lax.axis_index("ia")
    if count == 4:
        x, y = lax.rem(me, 2), me // 2
        x_near, y_near, far = me + 1 - 2 * x, me + 2 - 4 * y, 3 - me
        peers = [x_near, y_near]
    else:
        peers = [lax.rem(me + 1 + s, count) for s in range(count - 1)]

    def load(step):
        return pltpu.make_async_copy(
            t_ref.at[:, pl.ds(step * strip, strip)], tiles.at[step % 2], load_sems.at[step % 2]
        )

    def push(source, step, slot, target):
        copy = pltpu.make_async_remote_copy(
            parts.at[step, source], landed.at[step, slot], send.at[step, slot], recv.at[step, slot],
            device_id={"ia": target}, device_id_type=MESH,
        )
        copy.start()
        return copy

    load(0).start()
    line = lax.broadcasted_iota(jnp.int32, perm.shape, 0)
    lane = lax.broadcasted_iota(jnp.int32, perm.shape, 1)
    perm[...] = jnp.where(
        lane == lax.rem(line, group) * slices + lax.div(line, group), 1.0, 0.0
    ).astype(BF16)
    greet([{"ia": peer} for peer in peers])
    copies = {}

    def near(step):
        return (x_near, y_near) if step % 2 == 0 else (y_near, x_near)

    def relay(step):
        second = near(step)[1]
        copies[step, 1].wait_recv()
        added = parts[step, second].astype(F32) + landed[step, 1].astype(F32)
        parts[step, second] = added.astype(BF16)
        copies[step, 2] = push(second, step, 2, second)

    def finish(step):
        slots = (0, 2) if count == 4 else range(count - 1)
        total = parts[step, me].astype(F32)
        for slot in slots:
            copies[step, slot].wait_recv()
            total = total + landed[step, slot].astype(F32)
        for k in range(slices):
            out_ref[:, k, pl.ds(step * strip, strip)] = total[:, k * strip:(k + 1) * strip]

    for step in range(steps):
        if step + 1 < steps:
            load(step + 1).start()
        load(step).wait()

        @pl.loop(0, rows // group, unroll=4)
        def _(index):
            span = group * slices
            lines = pl.ds(pl.multiple_of(index * span, span), span)
            value = jnp.dot(perm[...], tiles[step % 2, lines, :], preferred_element_type=F32)
            value = value.astype(BF16)
            for k in range(slices):
                place = pl.ds(pl.multiple_of(index * group, group), group)
                turned[k, place, :] = value[k * group:(k + 1) * group]

        @pl.loop(0, slices, unroll=2)
        def _(k):
            value = jnp.dot(half_ref[...], turned[k], preferred_element_type=F32).astype(BF16)
            cols = pl.ds(pl.multiple_of(k * strip, strip), strip)
            parts[step, :, :, cols] = value.reshape(count, kept, strip)

        if count == 4:
            first = near(step)[0]
            copies[step, 1] = push(far, step, 1, first)
            copies[step, 0] = push(first, step, 0, first)
            if step >= 1:
                relay(step - 1)
        else:
            for s, peer in enumerate(peers):
                copies[step, s] = push(peer, step, s, peer)
        if step >= 4:
            finish(step - 4)
    if count == 4:
        relay(steps - 1)
    for step in range(max(steps - 4, 0), steps):
        finish(step)
    for copy in copies.values():
        copy.wait_send()


def project(tensor, half, count):
    rows, slices, columns = tensor.shape
    width = half.shape[0]
    kept = width // count
    strip = 256
    steps = columns // strip
    group = max(256 // slices, 16)
    return pl.pallas_call(
        functools.partial(project_kernel, count),
        out_shape=jax.ShapeDtypeStruct((kept, slices, columns), F32),
        in_specs=[pl.BlockSpec(memory_space=pl.ANY), pl.BlockSpec(memory_space=pltpu.VMEM)],
        out_specs=pl.BlockSpec(memory_space=pltpu.VMEM),
        scratch_shapes=[
            pltpu.VMEM((2, rows * slices, strip), BF16),
            pltpu.VMEM((group * slices, group * slices), BF16),
            pltpu.VMEM((slices, rows, strip), BF16),
            pltpu.VMEM((steps, count, kept, slices * strip), BF16),
            pltpu.VMEM((steps, count, kept, slices * strip), BF16),
            pltpu.SemaphoreType.DMA((2,)),
            pltpu.SemaphoreType.DMA((steps, count)),
            pltpu.SemaphoreType.DMA((steps, count)),
        ],
        compiler_params=pltpu.CompilerParams(
            collective_id=2, has_side_effects=True, vmem_limit_bytes=48 * MIB
        ),
        cost_estimate=pl.CostEstimate(
            flops=2 * rows * slices * columns * width,
            bytes_accessed=2 * rows * slices * columns, transcendentals=0,
        ),
    )(tensor.reshape(rows * slices, columns), half)


def shards(tensor, factor_j, factor_k):
    count, depth = lax.axis_size("ia"), lax.axis_size("ka")
    sketch, gram = sketch_sum(tensor, factor_j, factor_k, count, depth)
    basis = apply_factor(gram, sketch, False, F32)
    half = apply_factor(gram_sum(basis, count), basis, True, BF16)
    return project(tensor, half, count)


def solution(mesh):
    return jax.shard_map(
        shards,
        mesh=mesh,
        in_specs=(P("ia", "ka", "ja"), P("ja", None), P("ka", None)),
        out_specs=P("ia", "ka", "ja"),
        check_vma=False,
    )
```
